512 devices in a mesh: ctx: 64 (over x, z_lo, core), tp: 8 (over z_hi, y).
Axes of the slice: x: 4, y: 4, z: 16 (z_hi: 2, z_lo: 8; z = z_hi * 8 + z_lo), core: 2. Of those that a mesh axis runs over, the one named last changes fastest.
Arguments:
- states: bfloat16 [4096, 8192], P(None, 'ctx'), may hold values from -6 to 6
- qkv: bfloat16 [4096, 6144], P('ctx', 'tp'), may hold values from -40 to 40
- grad_out: bfloat16 [4096, 4096], P('ctx', 'tp'), may hold values from -6 to 6
- weight: bfloat16 [8192, 6144], P('ctx', 'tp'), may hold values from -0.0625 to 0.0625
- offsets: int32 [128], replicated, may hold values from 0 to 4064, as said below
Outputs:
- grad_states: bfloat16 [4096, 8192], P(None, 'ctx')
- grad_weight: float32 [8192, 6144], P('ctx', 'tp')
The draws below stay inside these ranges and needn't reach their ends.
Inputs may be any that keep to these rules, and one draw needn't show every extreme that they name: `offsets`: for each index i of ctx the two slabs are some slab p and slab 2 * 64 - 1 - p, each slab once, times 32.
All inputs are finite; a program needn't handle non-finite values.
Results may differ from the reference program's by a relative error of at most 0.017.
Values may be sent and summed in bfloat16 or wider, within the bound.
No kernel may reach another device: no remote copies, remote signals or barrier semaphores. Data moves between devices by JAX's collectives and lax.ppermute only.
A program may use at most 64 MiB of HBM per device.

```python
import jax
import jax.numpy as jnp
from jax import lax

D = 8192
HEADS = 32
KV_HEADS = 8
HEAD_DIM = 128
TOK_DEV = 64
SLAB = 32
TOKENS = 4096
COLUMNS = 6144
N_CTX = 64
N_TP = 8


def draw_qkv(key, part):
    key = jax.random.fold_in(key, 11)
    group = HEADS // KV_HEADS
    first = jax.random.fold_in(key, 0)
    shape = (TOKENS, KV_HEADS, group + 2, HEAD_DIM)
    full = jnp.clip(jax.random.normal(first, shape, jnp.float32), -4.0, 4.0)
    return full.reshape(TOKENS, (group + 2) * KV_HEADS * HEAD_DIM).astype(jnp.bfloat16)


def draw_offsets(key, part):
    key = jax.random.fold_in(key, 5)
    order = jax.random.permutation(key, N_CTX).astype(jnp.int32)
    paired = jnp.stack([order, 2 * N_CTX - 1 - order], axis=1).reshape(-1)
    return (paired * SLAB).astype(jnp.int32)


def levels(rng, dims, cuts, least, largest):
    def one(position, parts):
        steps = jax.random.uniform(jax.random.fold_in(jax.random.fold_in(rng, 6), position), (parts,), jnp.float32, least / len(cuts), largest / len(cuts))
        return jnp.repeat(jnp.exp(steps), dims[position] // parts).reshape((-1,) + (1,) * (len(dims) - position - 1))

    gain = one(*cuts[0])
    for cut in cuts[1:]:
        gain = gain * one(*cut)
    return gain


def gaussian(rng, shape, scale, limit, pieces=(), kind=jnp.bfloat16):
    level = levels(rng, shape, pieces, -0.22, 0.18) if pieces else 1.0
    array = jax.random.normal(rng, shape, jnp.float32) * scale * level
    return jnp.minimum(jnp.maximum(array, -limit), limit).astype(kind)


def setup_inputs(seed: int = 0) -> dict:
    streams_of = jax.random.split(jax.random.key(seed), 6)
    return {
        "states": gaussian(streams_of[0], (TOKENS, D), 1.0, 6.0, ((1, 64),)),
        "qkv": draw_qkv(jax.random.fold_in(streams_of[5], 71), 0),
        "grad_out": gaussian(streams_of[2], (TOKENS, HEADS * HEAD_DIM), 1.0, 6.0, ((0, 64), (1, 8))),
        "weight": gaussian(streams_of[3], (D, COLUMNS), D ** -0.5, 0.0625, ((0, 64), (1, 8))),
        "offsets": draw_offsets(jax.random.fold_in(streams_of[5], 71), 0),
    }


def reference(states, qkv, grad_out, weight, offsets):
    group = HEADS // KV_HEADS
    scale = HEAD_DIM ** -0.5
    steps_arr = jnp.arange(SLAB, dtype=jnp.int32)
    pos = (offsets[:, None] + steps_arr[None, :]).reshape(-1).astype(jnp.int32)
    blocks = qkv.reshape(TOKENS, KV_HEADS, group + 2, HEAD_DIM)
    queries = jnp.moveaxis(blocks[:, :, :group], 1, 0)
    keys = jnp.moveaxis(blocks[:, :, group], 1, 0)
    values = jnp.moveaxis(blocks[:, :, group + 1], 1, 0)
    grads = jnp.moveaxis(grad_out.reshape(TOKENS, KV_HEADS, group, HEAD_DIM), 1, 0)
    block_pos = pos.reshape(N_CTX, TOK_DEV)

    def one_group(items):
        query, key_rows, value_rows, cotangent = items
        kf = key_rows.astype(jnp.float32)
        vf = value_rows.astype(jnp.float32)
        query_blocks = query.reshape(N_CTX, TOK_DEV, group, HEAD_DIM)
        grad_blocks = cotangent.reshape(N_CTX, TOK_DEV, group, HEAD_DIM)

        def step(carry, xs):
            dkey_acc, dvalue_acc = carry
            q_blk, g_blk, p_blk = xs
            qf = q_blk.astype(jnp.float32)
            gf = g_blk.astype(jnp.float32)
            visible = pos[None, :] <= p_blk[:, None]
            scores = jnp.einsum('tgd,sd->gts', qf, kf) * scale
            scores = jnp.where(visible[None], scores, -jnp.inf)
            top = jnp.max(scores, axis=-1, keepdims=True)
            expd = jnp.exp(scores - top)
            probs = expd / jnp.sum(expd, axis=-1, keepdims=True)
            pb = lax.optimization_barrier(probs.astype(jnp.bfloat16)).astype(jnp.float32)
            output = jnp.einsum('gts,sd->tgd', pb, vf)
            delta = jnp.sum(gf * output, axis=-1)
            dprob = jnp.einsum('tgd,sd->gts', gf, vf)
            dscore = lax.optimization_barrier((probs * (dprob - delta.T[:, :, None]) * scale).astype(jnp.bfloat16)).astype(jnp.float32)
            dquery = jnp.einsum('gts,sd->tgd', dscore, kf).astype(jnp.bfloat16)
            dkey_acc = dkey_acc + jnp.einsum('gts,tgd->sd', dscore, qf)
            dvalue_acc = dvalue_acc + jnp.einsum('gts,tgd->sd', pb, gf)
            return (dkey_acc, dvalue_acc), dquery

        start = (jnp.zeros((TOKENS, HEAD_DIM), jnp.float32), jnp.zeros((TOKENS, HEAD_DIM), jnp.float32))
        (dkey, dvalue), dquery = lax.scan(step, start, (query_blocks, grad_blocks, block_pos))
        return dquery.reshape(TOKENS, group, HEAD_DIM), dkey.astype(jnp.bfloat16), dvalue.astype(jnp.bfloat16)

    dquery, dkey, dvalue = lax.map(one_group, (queries, keys, values, grads))
    joined = jnp.concatenate([dquery, dkey[:, :, None], dvalue[:, :, None]], axis=2)
    dqkv = jnp.moveaxis(joined, 0, 1).reshape(TOKENS, COLUMNS)
    share = COLUMNS // N_TP
    total = jnp.zeros((TOKENS, D), jnp.float32)
    for part_index in range(N_TP):
        left = dqkv[:, part_index * share:(part_index + 1) * share]
        right = weight[:, part_index * share:(part_index + 1) * share]
        term = jnp.dot(left, right.T, preferred_element_type=jnp.float32).astype(jnp.bfloat16)
        total = total + term.astype(jnp.float32)
    grad_states = total.astype(jnp.bfloat16)
    grad_weight = jnp.dot(states.T, dqkv, preferred_element_type=jnp.float32)
    return grad_states, grad_weight
```

```python
import functools

import jax
import jax.numpy as jnp
from jax import lax
from jax.experimental import pallas as pl
from jax.experimental.pallas import tpu as pltpu
from jax.sharding import Mesh
from jax.sharding import PartitionSpec as P

HEADS = 32
KV_HEADS = 8
HEAD_DIM = 128
GROUP = HEADS // KV_HEADS
X, Z, C, W, Y = 4, 8, 2, 2, 4
CHUNK = 512
BF = jnp.bfloat16
F32 = jnp.float32


def dot(a, b, contract):
    return lax.dot_general(a, b, (contract, ((), ())), preferred_element_type=F32)


def attention_kernel(q_ref, g_ref, own_ref, other_ref, qpos_ref, kpos_ref, dq_ref, down_ref, dother_ref, s_ref):
    half = own_ref.shape[0]
    steps = half // CHUNK
    scale = HEAD_DIM ** (-0.5)
    q = q_ref[...]
    g = g_ref[...]
    qpos = qpos_ref[...]
    rows = q.shape[0]
    sides = ((own_ref, down_ref), (other_ref, dother_ref))

    top = jnp.full((1, rows), -jnp.inf, F32)
    for side, (kv_ref, _) in enumerate(sides):
        for n in range(steps):
            at = n * CHUNK
            keys = kv_ref[at : at + CHUNK, :HEAD_DIM]
            scores = dot(keys, q, ((1,), (1,))) * scale
            visible = kpos_ref[side * half + at : side * half + at + CHUNK, :] <= qpos
            scores = jnp.where(visible, scores, -jnp.inf)
            s_ref[side * half + at : side * half + at + CHUNK, :] = scores
            top = jnp.maximum(top, jnp.max(scores, axis=0, keepdims=True))

    total = jnp.zeros((1, rows), F32)
    for n in range(2 * steps):
        at = n * CHUNK
        expd = jnp.exp(s_ref[at : at + CHUNK, :] - top)
        s_ref[at : at + CHUNK, :] = expd
        total = total + jnp.sum(expd, axis=0, keepdims=True)
    inverse = 1.0 / total

    output = jnp.zeros((HEAD_DIM, rows), F32)
    for side, (kv_ref, dkv_ref) in enumerate(sides):
        for n in range(steps):
            at = n * CHUNK
            values = kv_ref[at : at + CHUNK, HEAD_DIM:]
            probs = s_ref[side * half + at : side * half + at + CHUNK, :] * inverse
            s_ref[side * half + at : side * half + at + CHUNK, :] = probs
            rounded = probs.astype(BF)
            output = output + dot(values, rounded, ((0,), (0,)))
            dkv_ref[at : at + CHUNK, HEAD_DIM:] = dot(rounded, g, ((1,), (0,))).astype(dkv_ref.dtype)
    delta = jnp.sum(output * g.astype(F32).T, axis=0, keepdims=True)

    dquery = jnp.zeros((HEAD_DIM, rows), F32)
    for side, (kv_ref, dkv_ref) in enumerate(sides):
        for n in range(steps):
            at = n * CHUNK
            keys = kv_ref[at : at + CHUNK, :HEAD_DIM]
            values = kv_ref[at : at + CHUNK, HEAD_DIM:]
            dprob = dot(values, g, ((1,), (1,)))
            probs = s_ref[side * half + at : side * half + at + CHUNK, :]
            dscore = (probs * (dprob - delta) * scale).astype(BF)
            dquery = dquery + dot(keys, dscore, ((0,), (0,)))
            dkv_ref[at : at + CHUNK, :HEAD_DIM] = dot(dscore, q, ((1,), (0,))).astype(dkv_ref.dtype)
    dq_ref[...] = dquery.T.astype(BF)


def attention(q, g, own, other, qpos, kpos, interpret=False):
    rows = q.shape[0]
    half = own.shape[0]
    vmem = pl.BlockSpec(memory_space=pltpu.VMEM)
    return pl.pallas_call(
        attention_kernel,
        out_shape=(
            jax.ShapeDtypeStruct((rows, HEAD_DIM), BF),
            jax.ShapeDtypeStruct((half, 2 * HEAD_DIM), F32),
            jax.ShapeDtypeStruct((half, 2 * HEAD_DIM), BF),
        ),
        in_specs=[vmem] * 6,
        out_specs=(vmem,) * 3,
        scratch_shapes=[pltpu.VMEM((2 * half, rows), F32)],
        compiler_params=pltpu.CompilerParams(vmem_limit_bytes=40 * 1024 * 1024),
        interpret=interpret,
    )(q, g, own, other, qpos, kpos)


def gather(x, axis, size):
    copies = jnp.broadcast_to(x[None], (size,) + x.shape)
    return lax.all_to_all(copies, axis, 0, 0, tiled=True)


def swap(x, axis):
    return lax.ppermute(x, axis, [(0, 1), (1, 0)])


def body(states, qkv, grad_out, weight, offsets):
    rows, columns = qkv.shape
    half = rows // 2
    core = lax.axis_index("c")
    place = lax.axis_index("x") * (Z * C) + lax.axis_index("z") * C + core
    slab = jnp.arange(half, dtype=jnp.int32)
    mine = lax.dynamic_slice_in_dim(offsets, place * 2, 2)
    query_pos = (mine[:, None] + slab[None, :]).reshape(rows)
    query_pos = jnp.repeat(query_pos, GROUP)[None, :]
    key_off = jnp.moveaxis(offsets.reshape(X * Z, C, 2), 1, 0)
    key_off = jnp.where(core == 0, key_off, key_off[::-1])
    key_pos = (key_off.reshape(-1)[:, None] + slab[None, :]).reshape(-1, 1)

    wide = GROUP * HEAD_DIM
    pairs = qkv[:, wide:]
    pairs_z = gather(pairs, "z", Z)
    own = gather(pairs_z, "x", X).reshape(X * Z * rows, 2 * HEAD_DIM)
    other = swap(own, "c")

    q = qkv[:, :wide].reshape(rows * GROUP, HEAD_DIM)
    g = grad_out.reshape(rows * GROUP, HEAD_DIM)
    dq, dkv_own, dkv_other = attention(q, g, own, other, query_pos, key_pos)

    dkv = dkv_own + swap(dkv_other, "c").astype(F32)
    dkv = lax.all_to_all(dkv.astype(BF).reshape(X, Z * rows, 2 * HEAD_DIM), "x", 0, 0, tiled=True)
    dkv = jnp.sum(dkv.astype(F32), axis=0).astype(BF)
    dkv = lax.all_to_all(dkv.reshape(Z, rows, 2 * HEAD_DIM), "z", 0, 0, tiled=True)
    dkv = jnp.sum(dkv.astype(F32), axis=0).astype(BF)

    grads = jnp.concatenate([dq.reshape(rows, wide), dkv], axis=1)
    grads = gather(grads, "z", Z)
    grads_own = gather(grads, "x", X).reshape(X * Z * rows, columns)
    grads_other = swap(grads_own, "c")

    depth = weight.shape[0]
    part_own = dot(grads_own, weight, ((1,), (1,))).astype(BF).reshape(X * Z, rows, depth)
    part_other = dot(grads_other, weight, ((1,), (1,))).astype(BF).reshape(X * Z, rows, depth)
    first = jnp.where(core == 0, part_own, part_other)
    second = jnp.where(core == 0, part_other, part_own)
    part = jnp.stack([first, second], axis=1).reshape(Y, X * Z * C * rows // Y, depth)
    part = lax.all_to_all(part, "y", 0, 0, tiled=True)
    part = jnp.sum(part.astype(F32), axis=0).astype(BF)
    part = (part.astype(F32) + swap(part, "w").astype(F32)).astype(BF)
    grad_states = gather(part, "y", Y).reshape(X * Z * C * rows, depth)

    split = states.reshape(X * Z, C, rows, depth)
    states_own = lax.dynamic_index_in_dim(split, core, 1, keepdims=False).reshape(-1, depth)
    states_other = lax.dynamic_index_in_dim(split, 1 - core, 1, keepdims=False).reshape(-1, depth)
    grad_weight = dot(states_own, grads_own, ((0,), (0,))) + dot(states_other, grads_other, ((0,), (0,)))
    return grad_states, grad_weight


def solution(mesh):
    fine = Mesh(mesh.devices.reshape(X, Z, C, W, Y), ("x", "z", "c", "w", "y"))
    ctx, tp = ("x", "z", "c"), ("w", "y")
    return jax.shard_map(
        body,
        mesh=fine,
        in_specs=(P(None, ctx), P(ctx, tp), P(ctx, tp), P(ctx, tp), P()),
        out_specs=(P(None, ctx), P(ctx, tp)),
        check_vma=False,
    )
```

```python
import functools

import jax
import jax.numpy as jnp
from jax import lax
from jax.experimental import pallas as pl
from jax.experimental.pallas import tpu as pltpu
from jax.sharding import Mesh
from jax.sharding import PartitionSpec as P

HEADS = 32
KV_HEADS = 8
HEAD_DIM = 128
GROUP = HEADS // KV_HEADS
X, Z, C, W, Y = 4, 8, 2, 2, 4
CHUNK = 512
BF = jnp.bfloat16
F32 = jnp.float32


def dot(a, b, contract):
    return lax.dot_general(a, b, (contract, ((), ())), preferred_element_type=F32)


def attention_kernel(q_ref, g_ref, own_ref, other_ref, qpos_ref, kpos_ref, dq_ref, down_ref, dother_ref, s_ref):
    half = own_ref.shape[0]
    steps = half // CHUNK
    scale = HEAD_DIM ** (-0.5)
    q = q_ref[...]
    g = g_ref[...]
    qpos = qpos_ref[...]
    rows = q.shape[0]
    sides = ((own_ref, down_ref), (other_ref, dother_ref))

    top = jnp.full((1, rows), -jnp.inf, F32)
    for side, (kv_ref, _) in enumerate(sides):
        for n in range(steps):
            at = n * CHUNK
            keys = kv_ref[at : at + CHUNK, :HEAD_DIM]
            scores = dot(keys, q, ((1,), (1,))) * scale
            visible = kpos_ref[side * half + at : side * half + at + CHUNK, :] <= qpos
            scores = jnp.where(visible, scores, -jnp.inf)
            s_ref[side * half + at : side * half + at + CHUNK, :] = scores
            top = jnp.maximum(top, jnp.max(scores, axis=0, keepdims=True))

    total = jnp.zeros((1, rows), F32)
    for n in range(2 * steps):
        at = n * CHUNK
        expd = jnp.exp(s_ref[at : at + CHUNK, :] - top)
        s_ref[at : at + CHUNK, :] = expd
        total = total + jnp.sum(expd, axis=0, keepdims=True)
    inverse = 1.0 / total

    output = jnp.zeros((HEAD_DIM, rows), F32)
    for side, (kv_ref, dkv_ref) in enumerate(sides):
        for n in range(steps):
            at = n * CHUNK
            values = kv_ref[at : at + CHUNK, HEAD_DIM:]
            probs = s_ref[side * half + at : side * half + at + CHUNK, :] * inverse
            s_ref[side * half + at : side * half + at + CHUNK, :] = probs
            rounded = probs.astype(BF)
            output = output + dot(values, rounded, ((0,), (0,)))
            dkv_ref[at : at + CHUNK, HEAD_DIM:] = dot(rounded, g, ((1,), (0,))).astype(dkv_ref.dtype)
    delta = jnp.sum(output * g.astype(F32).T, axis=0, keepdims=True)

    dquery = jnp.zeros((HEAD_DIM, rows), F32)
    for side, (kv_ref, dkv_ref) in enumerate(sides):
        for n in range(steps):
            at = n * CHUNK
            keys = kv_ref[at : at + CHUNK, :HEAD_DIM]
            values = kv_ref[at : at + CHUNK, HEAD_DIM:]
            dprob = dot(values, g, ((1,), (1,)))
            probs = s_ref[side * half + at : side * half + at + CHUNK, :]
            dscore = (probs * (dprob - delta) * scale).astype(BF)
            dquery = dquery + dot(keys, dscore, ((0,), (0,)))
            dkv_ref[at : at + CHUNK, :HEAD_DIM] = dot(dscore, q, ((1,), (0,))).astype(dkv_ref.dtype)
    dq_ref[...] = dquery.T.astype(BF)


def attention(q, g, own, other, qpos, kpos, interpret=False):
    rows = q.shape[0]
    half = own.shape[0]
    vmem = pl.BlockSpec(memory_space=pltpu.VMEM)
    return pl.pallas_call(
        attention_kernel,
        out_shape=(
            jax.ShapeDtypeStruct((rows, HEAD_DIM), BF),
            jax.ShapeDtypeStruct((half, 2 * HEAD_DIM), BF),
            jax.ShapeDtypeStruct((half, 2 * HEAD_DIM), BF),
        ),
        in_specs=[vmem] * 6,
        out_specs=(vmem,) * 3,
        scratch_shapes=[pltpu.VMEM((2 * half, rows), F32)],
        compiler_params=pltpu.CompilerParams(vmem_limit_bytes=40 * 1024 * 1024),
        interpret=interpret,
    )(q, g, own, other, qpos, kpos)


def project_kernel(at_ref, dq_own_ref, dq_other_ref, dkv_own_ref, dkv_other_ref, weight_ref, *out_refs):
    mine = at_ref[0]
    core = at_ref[1]
    target = at_ref[2]
    wide = GROUP * HEAD_DIM
    for k, out_ref in enumerate(out_refs):
        place = target ^ k
        for side, (dq_ref, dkv_ref) in enumerate(((dq_own_ref, dkv_own_ref), (dq_other_ref, dkv_other_ref))):
            part = dot(dq_ref[mine ^ place], weight_ref[:, :wide], ((1,), (1,)))
            part = part + dot(dkv_ref[place], weight_ref[:, wide:], ((1,), (1,)))
            out_ref[:, core ^ side] = part.astype(BF).reshape(out_ref.shape[0], out_ref.shape[2], part.shape[1])


def place_kernel(at_ref, *refs):
    out_ref = refs[-1]
    for k in range(Y):
        out_ref[at_ref[2] ^ k] = refs[k][...]


def weight_kernel(at_ref, dq_own_ref, dq_other_ref, dkv_own_ref, dkv_other_ref, states_ref, out_ref):
    mine = at_ref[0]
    core = at_ref[1]
    wide = GROUP * HEAD_DIM
    depth = out_ref.shape[0]
    dq_sum = jnp.zeros((depth, wide), F32)
    dkv_sum = jnp.zeros((depth, 2 * HEAD_DIM), F32)
    for k in range(X):
        place = mine ^ k
        for side, (dq_ref, dkv_ref) in enumerate(((dq_own_ref, dkv_own_ref), (dq_other_ref, dkv_other_ref))):
            rows = states_ref[place, :, core ^ side].reshape(dq_ref.shape[1], depth)
            dq_sum = dq_sum + dot(rows, dq_ref[k], ((0,), (0,)))
            dkv_sum = dkv_sum + dot(rows, dkv_ref[place], ((0,), (0,)))
    out_ref[:, :wide] = dq_sum
    out_ref[:, wide:] = dkv_sum


def local_call(kernel, count, shape, dtype, *operands):
    vmem = pl.BlockSpec(memory_space=pltpu.VMEM)
    return pl.pallas_call(
        kernel,
        out_shape=[jax.ShapeDtypeStruct(shape, dtype)] * count,
        in_specs=[pl.BlockSpec(memory_space=pltpu.SMEM)] + [vmem] * (len(operands) - 1),
        out_specs=[vmem] * count,
        compiler_params=pltpu.CompilerParams(vmem_limit_bytes=40 * 1024 * 1024),
    )(*operands)


def gather(x, axis, size):
    copies = jnp.broadcast_to(x[None], (size,) + x.shape)
    return lax.all_to_all(copies, axis, 0, 0, tiled=True)


def swap(x, axis, size=2, bit=1):
    return lax.ppermute(x, axis, [(n, n ^ bit) for n in range(size)])


def body(states, qkv, grad_out, weight, offsets):
    rows, columns = qkv.shape
    half = rows // 2
    wide = GROUP * HEAD_DIM
    pair = 2 * HEAD_DIM
    core = lax.axis_index("c")
    mine = lax.axis_index("x")
    place = mine * (Z * C) + lax.axis_index("h") * (Z // 2 * C) + lax.axis_index("l") * C + core
    slab = jnp.arange(half, dtype=jnp.int32)
    at = lax.dynamic_slice_in_dim(offsets, place * 2, 2)
    query_pos = (at[:, None] + slab[None, :]).reshape(rows)
    query_pos = jnp.repeat(query_pos, GROUP)[None, :]
    key_off = jnp.moveaxis(offsets.reshape(X * Z, C, 2), 1, 0)
    key_off = jnp.where(core == 0, key_off, key_off[::-1])
    key_pos = (key_off.reshape(-1)[:, None] + slab[None, :]).reshape(-1, 1)

    pairs_z = gather(qkv[:, wide:], ("h", "l"), Z)
    own = gather(pairs_z, "x", X).reshape(X * Z * rows, pair)
    other = swap(own, "c")

    q = qkv[:, :wide].reshape(rows * GROUP, HEAD_DIM)
    g = grad_out.reshape(rows * GROUP, HEAD_DIM)
    dq, dkv_own, dkv_other = attention(q, g, own, other, query_pos, key_pos)

    dkv_in = swap(dkv_other, "c")
    dq_z = gather(dq.reshape(rows, wide), ("h", "l"), Z).reshape(Z * rows, wide)
    dkv = (dkv_own.astype(F32) + dkv_in.astype(F32)).astype(BF).reshape(X, Z * rows, pair)
    blocks = [lax.dynamic_index_in_dim(dkv, mine ^ k, 0, keepdims=False) for k in range(X)]
    total = blocks[0].astype(F32)
    for k in range(1, X):
        total = total + swap(blocks[k], "x", X, k).astype(F32)
    dkv = total.astype(BF)
    dkv, dq_z = lax.optimization_barrier((dkv, dq_z))

    dq_x = [dq_z] + [swap(dq_z, "x", X, k) for k in range(1, X)]
    dkv = lax.all_to_all(dkv.reshape(2, Z // 2, rows, pair), "l", 1, 1, tiled=True)
    dkv = jnp.sum(dkv.astype(F32), axis=1).astype(BF)
    dkv = (dkv.astype(F32) + swap(dkv, "h").astype(F32)).astype(BF)
    dkv_z = jnp.moveaxis(gather(dkv, "l", Z // 2), 0, 1).reshape(Z * rows, pair)

    dkv_own = gather(dkv_z, "x", X)
    dq_own = jnp.stack(dq_x)
    dq_other = swap(dq_own, "c")
    dkv_other = swap(dkv_own, "c")

    depth = weight.shape[0]
    where = jnp.stack([mine, core, lax.axis_index("y")]).astype(jnp.int32)
    pieces = (where, dq_own, dq_other, dkv_own, dkv_other)
    parts = local_call(project_kernel, Y, (Z, C, rows, depth), BF, *pieces, weight)
    part = parts[0].astype(F32)
    for k in range(1, Y):
        part = part + swap(parts[k], "y", Y, k).astype(F32)
    part = part.astype(BF)
    part = (part.astype(F32) + swap(part, "w").astype(F32)).astype(BF).reshape(Z * C * rows, depth)
    shares = [part] + [swap(part, "y", Y, k) for k in range(1, Y)]
    (grad_states,) = local_call(place_kernel, 1, (Y,) + part.shape, BF, where, *shares)
    (grad_weight,) = local_call(
        weight_kernel, 1, (depth, columns), F32, *pieces, states.reshape(X, Z, C, rows, depth)
    )
    return grad_states.reshape(-1, depth), grad_weight


def solution(mesh):
    fine = Mesh(mesh.devices.reshape(X, 2, Z // 2, C, W, Y), ("x", "h", "l", "c", "w", "y"))
    ctx, tp = ("x", "h", "l", "c"), ("w", "y")
    return jax.shard_map(
        body,
        mesh=fine,
        in_specs=(P(None, ctx), P(ctx, tp), P(ctx, tp), P(ctx, tp), P()),
        out_specs=(P(None, ctx), P(ctx, tp)),
        check_vma=False,
    )
```

```python
import functools

import jax
import jax.numpy as jnp
from jax import lax
from jax.experimental import pallas as pl
from jax.experimental.pallas import tpu as pltpu
from jax.sharding import Mesh
from jax.sharding import PartitionSpec as P

HEADS = 32
KV_HEADS = 8
HEAD_DIM = 128
GROUP = HEADS // KV_HEADS
X, Z, C, W, Y = 4, 8, 2, 2, 4
LOWEST = -1e30
BF = jnp.bfloat16
F32 = jnp.float32


def dot(a, b, contract):
    return lax.dot_general(a, b, (contract, ((), ())), preferred_element_type=F32)


def heads_to_rows(ref, start):
    return jnp.concatenate([ref[:, start + n * HEAD_DIM : start + (n + 1) * HEAD_DIM] for n in range(GROUP)], axis=0)


def masked_scores(keys, q, kpos, qpos):
    scores = dot(keys, q, ((1,), (1,))) * HEAD_DIM ** (-0.5)
    return jnp.where(kpos <= qpos, scores, -jnp.inf)


def stats_kernel(own_ref, other_ref, kpos_ref, qpos_ref, *refs):
    out_ref = refs[X]
    wide = GROUP * HEAD_DIM
    half = own_ref.shape[0]
    for k in range(X):
        q = heads_to_rows(refs[k], 0)
        g = heads_to_rows(refs[k], wide)
        qpos = qpos_ref[k : k + 1, :]
        scores = [
            masked_scores(kv_ref[:, :HEAD_DIM], q, kpos_ref[side * half : (side + 1) * half, :], qpos)
            for side, kv_ref in enumerate((own_ref, other_ref))
        ]
        top = jnp.full(qpos.shape, LOWEST, F32)
        for part in scores:
            top = jnp.maximum(top, jnp.max(part, axis=0, keepdims=True))
        total = jnp.zeros(qpos.shape, F32)
        weighted = jnp.zeros(qpos.shape, F32)
        for part, kv_ref in zip(scores, (own_ref, other_ref)):
            expd = jnp.exp(part - top)
            total = total + jnp.sum(expd, axis=0, keepdims=True)
            dprob = dot(kv_ref[:, HEAD_DIM:], g, ((1,), (1,)))
            weighted = weighted + jnp.sum(expd * dprob, axis=0, keepdims=True)
        for n in range(X):
            out_ref[n, k : k + 1, :] = top
            out_ref[n, X + k : X + k + 1, :] = total
            out_ref[n, 2 * X + k : 2 * X + k + 1, :] = weighted
    for n in range(X):
        out_ref[n, 3 * X :, :] = jnp.zeros((X, out_ref.shape[2]), F32)


def grads_kernel(at_ref, stats_ref, own_ref, other_ref, kpos_ref, qpos_ref, *refs):
    qg_refs, dq_ref = refs[:X], refs[X]
    dkv_refs = refs[X + 1 : X + 3]
    dkv_sum_ref = refs[X + 3]
    mine = at_ref[0]
    scale = HEAD_DIM ** (-0.5)
    wide = GROUP * HEAD_DIM
    half, rows = own_ref.shape[0], dq_ref.shape[1]
    for k in range(X):
        stat = [[stats_ref[mine ^ d, n * X + (d ^ k) : n * X + (d ^ k) + 1, :] for n in range(3)] for d in range(X)]
        top = functools.reduce(jnp.maximum, [one[0] for one in stat])
        shift = [jnp.exp(one[0] - top) for one in stat]
        inverse = 1.0 / sum(one[1] * c for one, c in zip(stat, shift))
        delta = sum(one[2] * c for one, c in zip(stat, shift)) * inverse
        q = heads_to_rows(qg_refs[k], 0)
        g = heads_to_rows(qg_refs[k], wide)
        qpos = qpos_ref[k : k + 1, :]
        dquery = jnp.zeros((HEAD_DIM, q.shape[0]), F32)
        for side, kv_ref in enumerate((own_ref, other_ref)):
            keys = kv_ref[:, :HEAD_DIM]
            kpos = kpos_ref[side * half : (side + 1) * half, :]
            probs = jnp.exp(masked_scores(keys, q, kpos, qpos) - top) * inverse
            dprob = dot(kv_ref[:, HEAD_DIM:], g, ((1,), (1,)))
            dscore = (probs * (dprob - delta) * scale).astype(BF)
            dquery = dquery + dot(keys, dscore, ((0,), (0,)))
            dkey = dot(dscore, q, ((1,), (0,)))
            dvalue = dot(probs.astype(BF), g, ((1,), (0,)))
            if k > 0:
                dkey = dkey + dkv_sum_ref[side, :, :HEAD_DIM]
                dvalue = dvalue + dkv_sum_ref[side, :, HEAD_DIM:]
            if k < X - 1:
                dkv_sum_ref[side, :, :HEAD_DIM] = dkey
                dkv_sum_ref[side, :, HEAD_DIM:] = dvalue
            else:
                dkv_refs[side][:, :HEAD_DIM] = dkey.astype(BF)
                dkv_refs[side][:, HEAD_DIM:] = dvalue.astype(BF)
        dquery = dquery.T.astype(BF)
        for n in range(GROUP):
            dq_ref[mine ^ k, :, n * HEAD_DIM : (n + 1) * HEAD_DIM] = dquery[n * rows : (n + 1) * rows]


def attention_stats(own, other, kpos, qpos, qg, interpret=False):
    vmem = pl.BlockSpec(memory_space=pltpu.VMEM)
    return pl.pallas_call(
        stats_kernel,
        out_shape=jax.ShapeDtypeStruct((X, 4 * X, qpos.shape[1]), F32),
        in_specs=[vmem] * (4 + X),
        out_specs=vmem,
        compiler_params=pltpu.CompilerParams(vmem_limit_bytes=40 * 1024 * 1024),
        interpret=interpret,
    )(own, other, kpos, qpos, *qg)


def attention_grads(at, stats, own, other, kpos, qpos, qg, interpret=False):
    vmem = pl.BlockSpec(memory_space=pltpu.VMEM)
    dq_shape = jax.ShapeDtypeStruct((X, qg[0].shape[0], GROUP * HEAD_DIM), BF)
    return pl.pallas_call(
        grads_kernel,
        out_shape=[dq_shape] + [jax.ShapeDtypeStruct(own.shape, BF)] * 2,
        in_specs=[pl.BlockSpec(memory_space=pltpu.SMEM)] + [vmem] * (5 + X),
        out_specs=[vmem] * 3,
        scratch_shapes=[pltpu.VMEM((2,) + own.shape, F32)],
        compiler_params=pltpu.CompilerParams(vmem_limit_bytes=40 * 1024 * 1024),
        interpret=interpret,
    )(at, stats, own, other, kpos, qpos, *qg)


def project_kernel(at_ref, *refs):
    piece_refs, weight_ref, out_ref = refs[: 2 * X], refs[2 * X], refs[2 * X + 1]
    rows = out_ref.shape[3]
    for k in range(X):
        for side in range(C):
            part = dot(piece_refs[side * X + k][...], weight_ref[...], ((1,), (1,))).astype(BF)
            for n in range(Z):
                block = part[n * rows : (n + 1) * rows]
                out_ref[at_ref[0] ^ k, n % 2 * (Z // 2) + n // 2, at_ref[1] ^ side] = block


def weight_kernel(at_ref, *refs):
    piece_refs, states_ref, out_ref = refs[: 2 * X], refs[2 * X], refs[2 * X + 1]
    total = jnp.zeros(out_ref.shape, F32)
    for k in range(X):
        for side in range(C):
            place, core = at_ref[0] ^ k, at_ref[1] ^ side
            rows = [states_ref[place, n % 2 * (Z // 2) + n // 2, core] for n in range(Z)]
            total = total + dot(jnp.concatenate(rows, axis=0), piece_refs[side * X + k][...], ((0,), (0,)))
    out_ref[...] = total


def add_kernel(at_ref, mine_ref, other_ref, out_ref):
    total = (mine_ref[...].astype(F32) + other_ref[...].astype(F32)).astype(BF)
    for n in range(out_ref.shape[0]):
        out_ref[n] = total


def local_call(kernel, shape, dtype, *operands):
    vmem = pl.BlockSpec(memory_space=pltpu.VMEM)
    return pl.pallas_call(
        kernel,
        out_shape=jax.ShapeDtypeStruct(shape, dtype),
        in_specs=[pl.BlockSpec(memory_space=pltpu.SMEM)] + [vmem] * (len(operands) - 1),
        out_specs=vmem,
        compiler_params=pltpu.CompilerParams(vmem_limit_bytes=40 * 1024 * 1024),
    )(*operands)


def gather(x, axis, size):
    copies = jnp.broadcast_to(x[None], (size,) + x.shape)
    return lax.all_to_all(copies, axis, 0, 0, tiled=True)


def swap(x, axis, size=2, bit=1):
    return lax.ppermute(x, axis, [(n, n ^ bit) for n in range(size)])


def body(states, qkv, grad_out, weight, offsets):
    rows, columns = qkv.shape
    half = rows // 2
    wide = GROUP * HEAD_DIM
    pair = 2 * HEAD_DIM
    core = lax.axis_index("c")
    mine = lax.axis_index("x")
    high = lax.axis_index("h")
    deep = high * (Z // 2) + lax.axis_index("l")
    where = jnp.stack([mine, core]).astype(jnp.int32)
    slab = jnp.arange(half, dtype=jnp.int32)
    starts = offsets.reshape(X, Z, C, 2)
    row_start = lax.dynamic_index_in_dim(lax.dynamic_index_in_dim(starts, deep, 1, False), core, 1, False)
    row_start = jnp.stack([lax.dynamic_index_in_dim(row_start, mine ^ k, 0, False) for k in range(X)])
    query_pos = (row_start[:, :, None] + slab).reshape(X, rows)
    query_pos = jnp.tile(query_pos, (1, GROUP))
    key_start = lax.dynamic_index_in_dim(starts, mine, 0, False)
    key_start = jnp.stack([lax.dynamic_index_in_dim(key_start, core ^ k, 1, False) for k in range(C)])
    key_pos = (key_start.reshape(-1)[:, None] + slab[None, :]).reshape(-1, 1)

    qg = jnp.concatenate([qkv[:, :wide], grad_out], axis=1)
    pairs = qkv[:, wide:]
    qg, pairs, key_pos, query_pos = lax.optimization_barrier((qg, pairs, key_pos, query_pos))
    qg_x = [qg] + [swap(qg, "x", X, k) for k in range(1, X)]
    own = gather(pairs, ("h", "l"), Z).reshape(Z * rows, pair)
    own, *qg_x = lax.optimization_barrier((own, *qg_x))
    other = swap(own, "c")

    stats = attention_stats(own, other, key_pos, query_pos, qg_x)
    stats = lax.all_to_all(stats, "x", 0, 0, tiled=True)
    dq, dkv, dkv_give = attention_grads(where, stats, own, other, key_pos, query_pos, qg_x)

    dkv_in = swap(dkv_give, "c")
    dq = jnp.sum(lax.all_to_all(dq, "x", 0, 0, tiled=True).astype(F32), axis=0).astype(BF)
    dkv = (dkv.astype(F32) + dkv_in.astype(F32)).astype(BF)
    dkv, dq = lax.optimization_barrier((dkv, dq))
    dkv = lax.all_to_all(dkv.reshape(2, Z // 2, rows, pair), "l", 1, 1, tiled=True)
    dq_h = jnp.stack([dq, swap(dq, "h")])
    dq_h = jnp.where(high == 0, dq_h, dq_h[::-1])
    dkv = jnp.sum(dkv.astype(F32), axis=1).astype(BF)
    dkv, dq_h = lax.optimization_barrier((dkv, dq_h))
    dkv = (dkv.astype(F32) + swap(dkv, "h").astype(F32)).astype(BF)

    grads = gather(jnp.concatenate([dq_h, dkv], axis=2), "l", Z // 2).reshape(Z * rows, columns)
    pieces = [grads] + [swap(grads, "x", X, k) for k in range(1, X)]
    pieces = pieces + [swap(piece, "c") for piece in pieces]

    depth = weight.shape[0]
    part = local_call(project_kernel, (X, Z, C, rows, depth), BF, where, *pieces, weight)
    part = lax.all_to_all(part.reshape(Y, Z * C * rows, depth), "y", 0, 0, tiled=True)
    part = jnp.sum(part.astype(F32), axis=0).astype(BF)
    grad_weight = local_call(
        weight_kernel, (depth, columns), F32, where, *pieces, states.reshape(X, Z, C, rows, depth)
    )
    part = local_call(add_kernel, (Y,) + part.shape, BF, where, part, swap(part, "w"))
    part, grad_weight = lax.optimization_barrier((part, grad_weight))
    grad_states = lax.all_to_all(part, "y", 0, 0, tiled=True)
    return grad_states.reshape(-1, depth), grad_weight


def solution(mesh):
    fine = Mesh(mesh.devices.reshape(X, 2, Z // 2, C, W, Y), ("x", "h", "l", "c", "w", "y"))
    ctx, tp = ("x", "h", "l", "c"), ("w", "y")
    return jax.shard_map(
        body,
        mesh=fine,
        in_specs=(P(None, ctx), P(ctx, tp), P(ctx, tp), P(ctx, tp), P()),
        out_specs=(P(None, ctx), P(ctx, tp)),
        check_vma=False,
    )
```

```python
import functools

import jax
import jax.numpy as jnp
from jax import lax
from jax.experimental import pallas as pl
from jax.experimental.pallas import tpu as pltpu
from jax.sharding import Mesh
from jax.sharding import PartitionSpec as P

HEADS = 32
KV_HEADS = 8
HEAD_DIM = 128
GROUP = HEADS // KV_HEADS
X, Z, C, W, Y = 4, 8, 2, 2, 4
LOWEST = -1e30
BF = jnp.bfloat16
F32 = jnp.float32


def dot(a, b, contract):
    return lax.dot_general(a, b, (contract, ((), ())), preferred_element_type=F32)


def heads_to_rows(ref, start):
    return jnp.concatenate([ref[:, start + n * HEAD_DIM : start + (n + 1) * HEAD_DIM] for n in range(GROUP)], axis=0)


def masked_scores(keys, q, kpos, qpos):
    scores = dot(keys, q, ((1,), (1,))) * HEAD_DIM ** (-0.5)
    return jnp.where(kpos <= qpos, scores, -jnp.inf)


def stats_kernel(own_ref, other_ref, kpos_ref, qpos_ref, *refs):
    out_ref = refs[X]
    wide = GROUP * HEAD_DIM
    half = own_ref.shape[0]
    for k in range(X):
        q = heads_to_rows(refs[k], 0)
        g = heads_to_rows(refs[k], wide)
        qpos = qpos_ref[k : k + 1, :]
        scores = [
            masked_scores(kv_ref[:, :HEAD_DIM], q, kpos_ref[side * half : (side + 1) * half, :], qpos)
            for side, kv_ref in enumerate((own_ref, other_ref))
        ]
        top = jnp.full(qpos.shape, LOWEST, F32)
        for part in scores:
            top = jnp.maximum(top, jnp.max(part, axis=0, keepdims=True))
        total = jnp.zeros(qpos.shape, F32)
        weighted = jnp.zeros(qpos.shape, F32)
        for part, kv_ref in zip(scores, (own_ref, other_ref)):
            expd = jnp.exp(part - top)
            total = total + jnp.sum(expd, axis=0, keepdims=True)
            dprob = dot(kv_ref[:, HEAD_DIM:], g, ((1,), (1,)))
            weighted = weighted + jnp.sum(expd * dprob, axis=0, keepdims=True)
        for n in range(X):
            out_ref[n, k : k + 1, :] = top
            out_ref[n, X + k : X + k + 1, :] = total
            out_ref[n, 2 * X + k : 2 * X + k + 1, :] = weighted
    for n in range(X):
        out_ref[n, 3 * X :, :] = jnp.zeros((X, out_ref.shape[2]), F32)


def grads_kernel(at_ref, stats_ref, own_ref, other_ref, kpos_ref, qpos_ref, *refs):
    qg_refs, dq_ref = refs[:X], refs[X]
    dkv_refs = refs[X + 1 : X + 3]
    dkv_sum_ref = refs[X + 3]
    mine = at_ref[0]
    scale = HEAD_DIM ** (-0.5)
    wide = GROUP * HEAD_DIM
    half, rows = own_ref.shape[0], dq_ref.shape[1]
    for k in range(X):
        stat = [[stats_ref[mine ^ d, n * X + (d ^ k) : n * X + (d ^ k) + 1, :] for n in range(3)] for d in range(X)]
        top = functools.reduce(jnp.maximum, [one[0] for one in stat])
        shift = [jnp.exp(one[0] - top) for one in stat]
        inverse = 1.0 / sum(one[1] * c for one, c in zip(stat, shift))
        delta = sum(one[2] * c for one, c in zip(stat, shift)) * inverse
        q = heads_to_rows(qg_refs[k], 0)
        g = heads_to_rows(qg_refs[k], wide)
        qpos = qpos_ref[k : k + 1, :]
        dquery = jnp.zeros((HEAD_DIM, q.shape[0]), F32)
        for side, kv_ref in enumerate((own_ref, other_ref)):
            keys = kv_ref[:, :HEAD_DIM]
            kpos = kpos_ref[side * half : (side + 1) * half, :]
            probs = jnp.exp(masked_scores(keys, q, kpos, qpos) - top) * inverse
            dprob = dot(kv_ref[:, HEAD_DIM:], g, ((1,), (1,)))
            dscore = (probs * (dprob - delta) * scale).astype(BF)
            dquery = dquery + dot(keys, dscore, ((0,), (0,)))
            dkey = dot(dscore, q, ((1,), (0,)))
            dvalue = dot(probs.astype(BF), g, ((1,), (0,)))
            if k > 0:
                dkey = dkey + dkv_sum_ref[side, :, :HEAD_DIM]
                dvalue = dvalue + dkv_sum_ref[side, :, HEAD_DIM:]
            if k < X - 1:
                dkv_sum_ref[side, :, :HEAD_DIM] = dkey
                dkv_sum_ref[side, :, HEAD_DIM:] = dvalue
            else:
                dkv_refs[side][:, :HEAD_DIM] = dkey.astype(BF)
                dkv_refs[side][:, HEAD_DIM:] = dvalue.astype(BF)
        dquery = dquery.T.astype(BF)
        for n in range(GROUP):
            dq_ref[mine ^ k, :, n * HEAD_DIM : (n + 1) * HEAD_DIM] = dquery[n * rows : (n + 1) * rows]


def attention_stats(own, other, kpos, qpos, qg, interpret=False):
    vmem = pl.BlockSpec(memory_space=pltpu.VMEM)
    return pl.pallas_call(
        stats_kernel,
        out_shape=jax.ShapeDtypeStruct((X, 4 * X, qpos.shape[1]), F32),
        in_specs=[vmem] * (4 + X),
        out_specs=vmem,
        compiler_params=pltpu.CompilerParams(vmem_limit_bytes=40 * 1024 * 1024),
        interpret=interpret,
    )(own, other, kpos, qpos, *qg)


def attention_grads(at, stats, own, other, kpos, qpos, qg, interpret=False):
    vmem = pl.BlockSpec(memory_space=pltpu.VMEM)
    dq_shape = jax.ShapeDtypeStruct((X, qg[0].shape[0], GROUP * HEAD_DIM), BF)
    return pl.pallas_call(
        grads_kernel,
        out_shape=[dq_shape] + [jax.ShapeDtypeStruct(own.shape, BF)] * 2,
        in_specs=[pl.BlockSpec(memory_space=pltpu.SMEM)] + [vmem] * (5 + X),
        out_specs=[vmem] * 3,
        scratch_shapes=[pltpu.VMEM((2,) + own.shape, F32)],
        compiler_params=pltpu.CompilerParams(vmem_limit_bytes=40 * 1024 * 1024),
        interpret=interpret,
    )(at, stats, own, other, kpos, qpos, *qg)


def combine_kernel(at_ref, mine_ref, other_ref, out_ref):
    high = at_ref[2]
    pair = mine_ref.shape[2]
    wide = GROUP * HEAD_DIM
    for n in range(2):
        total = (mine_ref[n].astype(F32) + other_ref[n].astype(F32)).astype(BF)
        for copy in range(out_ref.shape[0]):
            out_ref[copy, n, :, wide:] = total
            out_ref[copy, high, :, n * pair : (n + 1) * pair] = mine_ref[2 + n]
            out_ref[copy, 1 - high, :, n * pair : (n + 1) * pair] = other_ref[2 + n]


def project_kernel(at_ref, *refs):
    piece_refs, weight_refs, out_ref = refs[:C], refs[C : C + X], refs[C + X]
    rows = out_ref.shape[4]
    for k in range(X):
        for side in range(C):
            part = dot(piece_refs[side][...], weight_refs[k][...], ((1,), (1,))).astype(BF)
            for n in range(Z):
                z = n % 2 * (Z // 2) + n // 2
                half, odd = z // (Z // Y), z % (Z // Y)
                out_ref[at_ref[0] ^ k, half, odd, at_ref[1] ^ side] = part[n * rows : (n + 1) * rows]


def weight_kernel(at_ref, *refs):
    piece_refs, states_refs, out_ref = refs[:C], refs[C : C + X], refs[C + X]
    for k in range(X):
        total = jnp.zeros(out_ref.shape[1:], F32)
        for side in range(C):
            states = [states_refs[k][n % 2 * (Z // 2) + n // 2, at_ref[1] ^ side] for n in range(Z)]
            total = total + dot(jnp.concatenate(states, axis=0), piece_refs[side][...], ((0,), (0,)))
        out_ref[at_ref[0] ^ k] = total.astype(out_ref.dtype)


def add_kernel(at_ref, mine_ref, other_ref, out_ref):
    total = (mine_ref[...].astype(F32) + other_ref[...].astype(F32)).astype(BF)
    for n in range(out_ref.shape[0]):
        out_ref[n] = total


def local_call(kernel, shape, dtype, *operands):
    vmem = pl.BlockSpec(memory_space=pltpu.VMEM)
    return pl.pallas_call(
        kernel,
        out_shape=jax.ShapeDtypeStruct(shape, dtype),
        in_specs=[pl.BlockSpec(memory_space=pltpu.SMEM)] + [vmem] * (len(operands) - 1),
        out_specs=vmem,
        compiler_params=pltpu.CompilerParams(vmem_limit_bytes=40 * 1024 * 1024),
    )(*operands)


def gather(x, axis, size):
    copies = jnp.broadcast_to(x[None], (size,) + x.shape)
    return lax.all_to_all(copies, axis, 0, 0, tiled=True)


def swap(x, axis, size=2, bit=1):
    return lax.ppermute(x, axis, [(n, n ^ bit) for n in range(size)])


def body(states, qkv, grad_out, weight, offsets):
    rows, columns = qkv.shape
    half = rows // 2
    wide = GROUP * HEAD_DIM
    pair = 2 * HEAD_DIM
    core = lax.axis_index("c")
    mine = lax.axis_index("x")
    high = lax.axis_index("h")
    deep = high * (Z // 2) + lax.axis_index("l")
    where = jnp.stack([mine, core, high]).astype(jnp.int32)
    slab = jnp.arange(half, dtype=jnp.int32)
    starts = offsets.reshape(X, Z, C, 2)
    row_start = lax.dynamic_index_in_dim(lax.dynamic_index_in_dim(starts, deep, 1, False), core, 1, False)
    row_start = jnp.stack([lax.dynamic_index_in_dim(row_start, mine ^ k, 0, False) for k in range(X)])
    query_pos = (row_start[:, :, None] + slab).reshape(X, rows)
    query_pos = jnp.tile(query_pos, (1, GROUP))
    key_start = lax.dynamic_index_in_dim(starts, mine, 0, False)
    key_start = jnp.stack([lax.dynamic_index_in_dim(key_start, core ^ k, 1, False) for k in range(C)])
    key_pos = (key_start.reshape(-1)[:, None] + slab[None, :]).reshape(-1, 1)

    qg = jnp.concatenate([qkv[:, :wide], grad_out], axis=1)
    pairs = qkv[:, wide:]
    qg_x = [qg] + [swap(qg, "x", X, k) for k in range(1, X)]
    own = gather(pairs, ("h", "l"), Z).reshape(Z * rows, pair)
    own, key_pos, query_pos, *qg_x = lax.optimization_barrier((own, key_pos, query_pos, *qg_x))
    other = swap(own, "c")

    stats = attention_stats(own, other, key_pos, query_pos, qg_x)
    stats = lax.all_to_all(stats, "x", 0, 0, tiled=True)
    dq, dkv, dkv_give = attention_grads(where, stats, own, other, key_pos, query_pos, qg_x)

    dkv_in = swap(dkv_give, "c")
    dq = jnp.sum(lax.all_to_all(dq, "x", 0, 0, tiled=True).astype(F32), axis=0).astype(BF)
    dkv = (dkv.astype(F32) + dkv_in.astype(F32)).astype(BF)
    dkv, dq, weight = lax.optimization_barrier((dkv, dq, weight))
    weights = [weight] + [swap(weight, "x", X, k) for k in range(1, X)]
    dkv = lax.all_to_all(dkv.reshape(2, Z // 2, rows, pair), "l", 1, 1, tiled=True)
    dkv = jnp.sum(dkv.astype(F32), axis=1).astype(BF)
    joint = jnp.concatenate([dkv, dq[None, :, :pair], dq[None, :, pair:]], axis=0)
    grads = local_call(combine_kernel, (Z // 2, 2, rows, columns), BF, where, joint, swap(joint, "h"))
    grads, states, *weights = lax.optimization_barrier((grads, states, *weights))

    grads = lax.all_to_all(grads, "l", 0, 0, tiled=True).reshape(Z * rows, columns)
    depth = weight.shape[0]
    blocks = states.reshape(X, Z, C, rows, depth)
    blocks = [lax.dynamic_index_in_dim(blocks, mine ^ k, 0, keepdims=False) for k in range(X)]
    blocks = [blocks[0]] + [swap(blocks[k], "x", X, k) for k in range(1, X)]
    grads, *blocks = lax.optimization_barrier((grads, *blocks))
    pieces = [grads, swap(grads, "c")]

    part = local_call(project_kernel, (X, Y, Z // Y, C, rows, depth), BF, where, *pieces, *weights)
    part = lax.all_to_all(part.reshape(X * Y, -1, depth), ("x", "y"), 0, 0, tiled=True)
    part = jnp.sum(part.reshape(X, Y, -1, depth).astype(F32), axis=1).astype(BF)
    grad_weight = local_call(weight_kernel, (X, depth, columns), BF, where, *pieces, *blocks)
    grad_weight = jnp.sum(lax.all_to_all(grad_weight, "x", 0, 0, tiled=True).astype(F32), axis=0)
    part = local_call(add_kernel, (Y,) + part.shape, BF, where, part, swap(part, "w"))
    part, grad_weight = lax.optimization_barrier((part, grad_weight))
    grad_states = lax.all_to_all(part, "y", 0, 0, tiled=True)
    return jnp.moveaxis(grad_states, 0, 1).reshape(-1, depth), grad_weight


def solution(mesh):
    fine = Mesh(mesh.devices.reshape(X, 2, Z // 2, C, W, Y), ("x", "h", "l", "c", "w", "y"))
    ctx, tp = ("x", "h", "l", "c"), ("w", "y")
    return jax.shard_map(
        body,
        mesh=fine,
        in_specs=(P(None, ctx), P(ctx, tp), P(ctx, tp), P(ctx, tp), P()),
        out_specs=(P(None, ctx), P(ctx, tp)),
        check_vma=False,
    )
```

```python
import functools

import jax
import jax.numpy as jnp
from jax import lax
from jax.experimental import pallas as pl
from jax.experimental.pallas import tpu as pltpu
from jax.sharding import Mesh
from jax.sharding import PartitionSpec as P

HEADS = 32
KV_HEADS = 8
HEAD_DIM = 128
GROUP = HEADS // KV_HEADS
X, Z, C, W, Y = 4, 8, 2, 2, 4
LOWEST = -1e30
BF = jnp.bfloat16
F32 = jnp.float32


def dot(a, b, contract):
    return lax.dot_general(a, b, (contract, ((), ())), preferred_element_type=F32)


def heads_to_rows(ref, start):
    return jnp.concatenate([ref[:, start + n * HEAD_DIM : start + (n + 1) * HEAD_DIM] for n in range(GROUP)], axis=0)


def masked_scores(keys, q, kpos, qpos):
    scores = dot(keys, q, ((1,), (1,))) * HEAD_DIM ** (-0.5)
    return jnp.where(kpos <= qpos, scores, -jnp.inf)


def stats_kernel(own_ref, other_ref, kpos_ref, qpos_ref, *refs):
    out_ref = refs[X]
    wide = GROUP * HEAD_DIM
    half = own_ref.shape[0]
    for k in range(X):
        q = heads_to_rows(refs[k], 0)
        g = heads_to_rows(refs[k], wide)
        qpos = qpos_ref[k : k + 1, :]
        scores = [
            masked_scores(kv_ref[:, :HEAD_DIM], q, kpos_ref[side * half : (side + 1) * half, :], qpos)
            for side, kv_ref in enumerate((own_ref, other_ref))
        ]
        top = jnp.full(qpos.shape, LOWEST, F32)
        for part in scores:
            top = jnp.maximum(top, jnp.max(part, axis=0, keepdims=True))
        total = jnp.zeros(qpos.shape, F32)
        weighted = jnp.zeros(qpos.shape, F32)
        for part, kv_ref in zip(scores, (own_ref, other_ref)):
            expd = jnp.exp(part - top)
            total = total + jnp.sum(expd, axis=0, keepdims=True)
            dprob = dot(kv_ref[:, HEAD_DIM:], g, ((1,), (1,)))
            weighted = weighted + jnp.sum(expd * dprob, axis=0, keepdims=True)
        for n in range(X):
            out_ref[n, k : k + 1, :] = top
            out_ref[n, X + k : X + k + 1, :] = total
            out_ref[n, 2 * X + k : 2 * X + k + 1, :] = weighted
    for n in range(X):
        out_ref[n, 3 * X :, :] = jnp.zeros((X, out_ref.shape[2]), F32)


def grads_kernel(at_ref, stats_ref, own_ref, other_ref, kpos_ref, qpos_ref, *refs):
    qg_refs, dq_ref = refs[:X], refs[X]
    dkv_refs = refs[X + 1 : X + 3]
    dkv_sum_ref = refs[X + 3]
    mine = at_ref[0]
    scale = HEAD_DIM ** (-0.5)
    wide = GROUP * HEAD_DIM
    half, rows = own_ref.shape[0], dq_ref.shape[1]
    for k in range(X):
        stat = [[stats_ref[mine ^ d, n * X + (d ^ k) : n * X + (d ^ k) + 1, :] for n in range(3)] for d in range(X)]
        top = functools.reduce(jnp.maximum, [one[0] for one in stat])
        shift = [jnp.exp(one[0] - top) for one in stat]
        inverse = 1.0 / sum(one[1] * c for one, c in zip(stat, shift))
        delta = sum(one[2] * c for one, c in zip(stat, shift)) * inverse
        q = heads_to_rows(qg_refs[k], 0)
        g = heads_to_rows(qg_refs[k], wide)
        qpos = qpos_ref[k : k + 1, :]
        dquery = jnp.zeros((HEAD_DIM, q.shape[0]), F32)
        for side, kv_ref in enumerate((own_ref, other_ref)):
            keys = kv_ref[:, :HEAD_DIM]
            kpos = kpos_ref[side * half : (side + 1) * half, :]
            probs = jnp.exp(masked_scores(keys, q, kpos, qpos) - top) * inverse
            dprob = dot(kv_ref[:, HEAD_DIM:], g, ((1,), (1,)))
            dscore = (probs * (dprob - delta) * scale).astype(BF)
            dquery = dquery + dot(keys, dscore, ((0,), (0,)))
            dkey = dot(dscore, q, ((1,), (0,)))
            dvalue = dot(probs.astype(BF), g, ((1,), (0,)))
            if k > 0:
                dkey = dkey + dkv_sum_ref[side, :, :HEAD_DIM]
                dvalue = dvalue + dkv_sum_ref[side, :, HEAD_DIM:]
            if k < X - 1:
                dkv_sum_ref[side, :, :HEAD_DIM] = dkey
                dkv_sum_ref[side, :, HEAD_DIM:] = dvalue
            else:
                dkv_refs[side][:, :HEAD_DIM] = dkey.astype(BF)
                dkv_refs[side][:, HEAD_DIM:] = dvalue.astype(BF)
        dquery = dquery.T.astype(BF)
        for n in range(GROUP):
            dq_ref[mine ^ k, :, n * HEAD_DIM : (n + 1) * HEAD_DIM] = dquery[n * rows : (n + 1) * rows]


def attention_stats(own, other, kpos, qpos, qg, interpret=False):
    vmem = pl.BlockSpec(memory_space=pltpu.VMEM)
    return pl.pallas_call(
        stats_kernel,
        out_shape=jax.ShapeDtypeStruct((X, 4 * X, qpos.shape[1]), F32),
        in_specs=[vmem] * (4 + X),
        out_specs=vmem,
        compiler_params=pltpu.CompilerParams(vmem_limit_bytes=40 * 1024 * 1024),
        interpret=interpret,
    )(own, other, kpos, qpos, *qg)


def attention_grads(at, stats, own, other, kpos, qpos, qg, interpret=False):
    vmem = pl.BlockSpec(memory_space=pltpu.VMEM)
    dq_shape = jax.ShapeDtypeStruct((X, qg[0].shape[0], GROUP * HEAD_DIM), BF)
    return pl.pallas_call(
        grads_kernel,
        out_shape=[dq_shape] + [jax.ShapeDtypeStruct(own.shape, BF)] * 2,
        in_specs=[pl.BlockSpec(memory_space=pltpu.SMEM)] + [vmem] * (5 + X),
        out_specs=[vmem] * 3,
        scratch_shapes=[pltpu.VMEM((2,) + own.shape, F32)],
        compiler_params=pltpu.CompilerParams(vmem_limit_bytes=40 * 1024 * 1024),
        interpret=interpret,
    )(at, stats, own, other, kpos, qpos, *qg)


def combine_kernel(at_ref, mine_ref, other_ref, out_ref):
    high = at_ref[2]
    pair = mine_ref.shape[2]
    wide = GROUP * HEAD_DIM
    for n in range(2):
        total = (mine_ref[n].astype(F32) + other_ref[n].astype(F32)).astype(BF)
        for copy in range(out_ref.shape[0]):
            out_ref[copy, n, :, wide:] = total
            out_ref[copy, high, :, n * pair : (n + 1) * pair] = mine_ref[2 + n]
            out_ref[copy, 1 - high, :, n * pair : (n + 1) * pair] = other_ref[2 + n]


def project_kernel(at_ref, *refs):
    piece_refs, weight_refs, out_ref = refs[:C], refs[C : C + X], refs[C + X]
    rows = out_ref.shape[4]
    for k in range(X):
        for side in range(C):
            part = dot(piece_refs[side][...], weight_refs[k][...], ((1,), (1,))).astype(BF)
            for n in range(Z):
                z = n % 2 * (Z // 2) + n // 2
                half, odd = z // (Z // Y), z % (Z // Y)
                out_ref[at_ref[0] ^ k, half, odd, at_ref[1] ^ side] = part[n * rows : (n + 1) * rows]


def weight_kernel(at_ref, *refs):
    piece_refs, states_refs, out_refs = refs[:C], refs[C : C + X], refs[C + X :]
    for k in range(X):
        total = jnp.zeros(out_refs[k].shape, F32)
        for side in range(C):
            states = [states_refs[k][n % 2 * (Z // 2) + n // 2, at_ref[1] ^ side] for n in range(Z)]
            total = total + dot(jnp.concatenate(states, axis=0), piece_refs[side][...], ((0,), (0,)))
        out_refs[k][...] = total.astype(out_refs[k].dtype)


def add_kernel(at_ref, mine_ref, other_ref, out_ref):
    total = (mine_ref[...].astype(F32) + other_ref[...].astype(F32)).astype(BF)
    for n in range(out_ref.shape[0]):
        out_ref[n] = total


def local_call(kernel, shape, dtype, *operands):
    vmem = pl.BlockSpec(memory_space=pltpu.VMEM)
    return pl.pallas_call(
        kernel,
        out_shape=jax.ShapeDtypeStruct(shape, dtype),
        in_specs=[pl.BlockSpec(memory_space=pltpu.SMEM)] + [vmem] * (len(operands) - 1),
        out_specs=vmem,
        compiler_params=pltpu.CompilerParams(vmem_limit_bytes=40 * 1024 * 1024),
    )(*operands)


def weight_call(shape, *operands):
    vmem = pl.BlockSpec(memory_space=pltpu.VMEM)
    return pl.pallas_call(
        weight_kernel,
        out_shape=[jax.ShapeDtypeStruct(shape, BF)] * X,
        in_specs=[pl.BlockSpec(memory_space=pltpu.SMEM)] + [vmem] * (len(operands) - 1),
        out_specs=[vmem] * X,
        compiler_params=pltpu.CompilerParams(vmem_limit_bytes=40 * 1024 * 1024),
    )(*operands)


def gather(x, axis, size):
    copies = jnp.broadcast_to(x[None], (size,) + x.shape)
    return lax.all_to_all(copies, axis, 0, 0, tiled=True)


def swap(x, axis, size=2, bit=1):
    return lax.ppermute(x, axis, [(n, n ^ bit) for n in range(size)])


def body(states, qkv, grad_out, weight, offsets):
    rows, columns = qkv.shape
    half = rows // 2
    wide = GROUP * HEAD_DIM
    pair = 2 * HEAD_DIM
    core = lax.axis_index("c")
    mine = lax.axis_index("x")
    high = lax.axis_index("h")
    deep = high * (Z // 2) + lax.axis_index("l")
    where = jnp.stack([mine, core, high]).astype(jnp.int32)
    slab = jnp.arange(half, dtype=jnp.int32)
    starts = offsets.reshape(X, Z, C, 2)
    row_start = lax.dynamic_index_in_dim(lax.dynamic_index_in_dim(starts, deep, 1, False), core, 1, False)
    row_start = jnp.stack([lax.dynamic_index_in_dim(row_start, mine ^ k, 0, False) for k in range(X)])
    query_pos = (row_start[:, :, None] + slab).reshape(X, rows)
    query_pos = jnp.tile(query_pos, (1, GROUP))
    key_start = lax.dynamic_index_in_dim(starts, mine, 0, False)
    key_start = jnp.stack([lax.dynamic_index_in_dim(key_start, core ^ k, 1, False) for k in range(C)])
    key_start = jnp.moveaxis(key_start.reshape(C, 2, Z // 2, 2), 1, 2)
    key_pos = (key_start.reshape(-1)[:, None] + slab[None, :]).reshape(-1, 1)

    qg = jnp.concatenate([qkv[:, :wide], grad_out], axis=1)
    pairs = qkv[:, wide:]
    qg_x = [qg] + [swap(qg, "x", X, k) for k in range(1, X)]
    own = gather(pairs, ("l", "h"), Z).reshape(Z * rows, pair)
    own, key_pos, query_pos, *qg_x = lax.optimization_barrier((own, key_pos, query_pos, *qg_x))
    other = swap(own, "c")

    stats = attention_stats(own, other, key_pos, query_pos, qg_x)
    stats = lax.all_to_all(stats, "x", 0, 0, tiled=True)
    dq, dkv, dkv_give = attention_grads(where, stats, own, other, key_pos, query_pos, qg_x)

    dkv_in = swap(dkv_give, "c")
    dq = jnp.sum(lax.all_to_all(dq, "x", 0, 0, tiled=True).astype(F32), axis=0).astype(BF)
    dkv = (dkv.astype(F32) + dkv_in.astype(F32)).astype(BF)
    dkv, dq, weight, states = lax.optimization_barrier((dkv, dq, weight, states))
    depth = weight.shape[0]
    blocks = states.reshape(X, Z, C, rows, depth)
    blocks = [lax.dynamic_index_in_dim(blocks, mine ^ k, 0, keepdims=False) for k in range(X)]
    blocks = [blocks[0]] + [swap(blocks[k], "x", X, k) for k in range(1, X)]
    dkv = lax.all_to_all(dkv.reshape(Z // 2, 2, rows, pair), "l", 0, 0, tiled=True)
    dkv = jnp.sum(dkv.astype(F32), axis=0).astype(BF)
    joint = jnp.concatenate([dkv, dq[None, :, :pair], dq[None, :, pair:]], axis=0)
    grads = local_call(combine_kernel, (Z // 2, 2, rows, columns), BF, where, joint, swap(joint, "h"))
    grads, weight, *blocks = lax.optimization_barrier((grads, weight, *blocks))
    weights = [weight] + [swap(weight, "x", X, k) for k in range(1, X)]

    grads = lax.all_to_all(grads, "l", 0, 0, tiled=True).reshape(Z * rows, columns)
    grads, *weights = lax.optimization_barrier((grads, *weights))
    pieces = [grads, swap(grads, "c")]

    part = local_call(project_kernel, (X, Y, Z // Y, C, rows, depth), BF, where, *pieces, *weights)
    part = lax.all_to_all(part.reshape(X * Y, -1, depth), ("x", "y"), 0, 0, tiled=True)
    part = jnp.sum(part.reshape(X, Y, -1, depth).astype(F32), axis=1).astype(BF)
    gw = weight_call((depth, columns), where, *pieces, *blocks)
    grad_weight = gw[0].astype(F32)
    for k in range(1, X):
        grad_weight = grad_weight + swap(gw[k], "x", X, k).astype(F32)
    part = local_call(add_kernel, (Y,) + part.shape, BF, where, part, swap(part, "w"))
    part, grad_weight = lax.optimization_barrier((part, grad_weight))
    grad_states = lax.all_to_all(part, "y", 0, 0, tiled=True)
    return jnp.moveaxis(grad_states, 0, 1).reshape(-1, depth), grad_weight


def solution(mesh):
    fine = Mesh(mesh.devices.reshape(X, 2, Z // 2, C, W, Y), ("x", "h", "l", "c", "w", "y"))
    ctx, tp = ("x", "h", "l", "c"), ("w", "y")
    return jax.shard_map(
        body,
        mesh=fine,
        in_specs=(P(None, ctx), P(ctx, tp), P(ctx, tp), P(ctx, tp), P()),
        out_specs=(P(None, ctx), P(ctx, tp)),
        check_vma=False,
    )
```

```python
import functools

import jax
import jax.numpy as jnp
from jax import lax
from jax.experimental import pallas as pl
from jax.experimental.pallas import tpu as pltpu
from jax.sharding import Mesh
from jax.sharding import PartitionSpec as P

HEADS = 32
KV_HEADS = 8
HEAD_DIM = 128
GROUP = HEADS // KV_HEADS
X, Z, C, W, Y = 4, 8, 2, 2, 4
LOWEST = -1e30
BF = jnp.bfloat16
F32 = jnp.float32


def dot(a, b, contract):
    return lax.dot_general(a, b, (contract, ((), ())), preferred_element_type=F32)


def heads_to_rows(ref, start):
    return jnp.concatenate([ref[:, start + n * HEAD_DIM : start + (n + 1) * HEAD_DIM] for n in range(GROUP)], axis=0)


def masked_scores(keys, q, kpos, qpos):
    scores = dot(keys, q, ((1,), (1,))) * HEAD_DIM ** (-0.5)
    return jnp.where(kpos <= qpos, scores, -jnp.inf)


def stats_kernel(own_ref, other_ref, kpos_ref, qpos_ref, *refs):
    out_ref = refs[X]
    wide = GROUP * HEAD_DIM
    half = own_ref.shape[0]
    for k in range(X):
        q = heads_to_rows(refs[k], 0)
        g = heads_to_rows(refs[k], wide)
        qpos = qpos_ref[k : k + 1, :]
        scores = [
            masked_scores(kv_ref[:, :HEAD_DIM], q, kpos_ref[side * half : (side + 1) * half, :], qpos)
            for side, kv_ref in enumerate((own_ref, other_ref))
        ]
        top = jnp.full(qpos.shape, LOWEST, F32)
        for part in scores:
            top = jnp.maximum(top, jnp.max(part, axis=0, keepdims=True))
        total = jnp.zeros(qpos.shape, F32)
        weighted = jnp.zeros(qpos.shape, F32)
        for part, kv_ref in zip(scores, (own_ref, other_ref)):
            expd = jnp.exp(part - top)
            total = total + jnp.sum(expd, axis=0, keepdims=True)
            dprob = dot(kv_ref[:, HEAD_DIM:], g, ((1,), (1,)))
            weighted = weighted + jnp.sum(expd * dprob, axis=0, keepdims=True)
        for n in range(X):
            out_ref[n, k : k + 1, :] = top
            out_ref[n, X + k : X + k + 1, :] = total
            out_ref[n, 2 * X + k : 2 * X + k + 1, :] = weighted
    for n in range(X):
        out_ref[n, 3 * X :, :] = jnp.zeros((X, out_ref.shape[2]), F32)


def grads_kernel(at_ref, stats_ref, own_ref, other_ref, kpos_ref, qpos_ref, *refs):
    qg_refs, dq_ref = refs[:X], refs[X]
    dkv_refs = refs[X + 1 : X + 3]
    dkv_sum_ref = refs[X + 3]
    mine = at_ref[0]
    scale = HEAD_DIM ** (-0.5)
    wide = GROUP * HEAD_DIM
    half, rows = own_ref.shape[0], dq_ref.shape[1]
    for k in range(X):
        stat = [[stats_ref[mine ^ d, n * X + (d ^ k) : n * X + (d ^ k) + 1, :] for n in range(3)] for d in range(X)]
        top = functools.reduce(jnp.maximum, [one[0] for one in stat])
        shift = [jnp.exp(one[0] - top) for one in stat]
        inverse = 1.0 / sum(one[1] * c for one, c in zip(stat, shift))
        delta = sum(one[2] * c for one, c in zip(stat, shift)) * inverse
        q = heads_to_rows(qg_refs[k], 0)
        g = heads_to_rows(qg_refs[k], wide)
        qpos = qpos_ref[k : k + 1, :]
        dquery = jnp.zeros((HEAD_DIM, q.shape[0]), F32)
        for side, kv_ref in enumerate((own_ref, other_ref)):
            keys = kv_ref[:, :HEAD_DIM]
            kpos = kpos_ref[side * half : (side + 1) * half, :]
            probs = jnp.exp(masked_scores(keys, q, kpos, qpos) - top) * inverse
            dprob = dot(kv_ref[:, HEAD_DIM:], g, ((1,), (1,)))
            dscore = (probs * (dprob - delta) * scale).astype(BF)
            dquery = dquery + dot(keys, dscore, ((0,), (0,)))
            dkey = dot(dscore, q, ((1,), (0,)))
            dvalue = dot(probs.astype(BF), g, ((1,), (0,)))
            if k > 0:
                dkey = dkey + dkv_sum_ref[side, :, :HEAD_DIM]
                dvalue = dvalue + dkv_sum_ref[side, :, HEAD_DIM:]
            if k < X - 1:
                dkv_sum_ref[side, :, :HEAD_DIM] = dkey
                dkv_sum_ref[side, :, HEAD_DIM:] = dvalue
            else:
                dkv_refs[side][:, :HEAD_DIM] = dkey.astype(BF)
                dkv_refs[side][:, HEAD_DIM:] = dvalue.astype(BF)
        dquery = dquery.T.astype(BF)
        for n in range(GROUP):
            dq_ref[mine ^ k, :, n * HEAD_DIM : (n + 1) * HEAD_DIM] = dquery[n * rows : (n + 1) * rows]


def attention_stats(own, other, kpos, qpos, qg, interpret=False):
    vmem = pl.BlockSpec(memory_space=pltpu.VMEM)
    return pl.pallas_call(
        stats_kernel,
        out_shape=jax.ShapeDtypeStruct((X, 4 * X, qpos.shape[1]), F32),
        in_specs=[vmem] * (4 + X),
        out_specs=vmem,
        compiler_params=pltpu.CompilerParams(vmem_limit_bytes=40 * 1024 * 1024),
        interpret=interpret,
    )(own, other, kpos, qpos, *qg)


def attention_grads(at, stats, own, other, kpos, qpos, qg, interpret=False):
    vmem = pl.BlockSpec(memory_space=pltpu.VMEM)
    dq_shape = jax.ShapeDtypeStruct((X, qg[0].shape[0], GROUP * HEAD_DIM), BF)
    return pl.pallas_call(
        grads_kernel,
        out_shape=[dq_shape] + [jax.ShapeDtypeStruct(own.shape, BF)] * 2,
        in_specs=[pl.BlockSpec(memory_space=pltpu.SMEM)] + [vmem] * (5 + X),
        out_specs=[vmem] * 3,
        scratch_shapes=[pltpu.VMEM((2,) + own.shape, F32)],
        compiler_params=pltpu.CompilerParams(vmem_limit_bytes=40 * 1024 * 1024),
        interpret=interpret,
    )(at, stats, own, other, kpos, qpos, *qg)


def combine_kernel(at_ref, mine_ref, other_ref, out_ref):
    high = at_ref[2]
    pair = mine_ref.shape[2]
    wide = GROUP * HEAD_DIM
    for n in range(2):
        total = (mine_ref[n].astype(F32) + other_ref[n].astype(F32)).astype(BF)
        for copy in range(out_ref.shape[0]):
            out_ref[copy, n, :, wide:] = total
            out_ref[copy, high, :, n * pair : (n + 1) * pair] = mine_ref[2 + n]
            out_ref[copy, 1 - high, :, n * pair : (n + 1) * pair] = other_ref[2 + n]


def project_kernel(at_ref, *refs):
    piece_refs, weight_refs, out_ref = refs[:C], refs[C : C + X], refs[C + X]
    rows = out_ref.shape[4]
    for k in range(X):
        for side in range(C):
            part = dot(piece_refs[side][...], weight_refs[k][...], ((1,), (1,))).astype(BF)
            for n in range(Z):
                z = n % 2 * (Z // 2) + n // 2
                half, odd = z // (Z // Y), z % (Z // Y)
                out_ref[at_ref[0] ^ k, half, odd, at_ref[1] ^ side] = part[n * rows : (n + 1) * rows]


def weight_kernel(at_ref, *refs):
    piece_refs, states_refs, out_refs = refs[:C], refs[C : C + X], refs[C + X :]
    for k in range(X):
        total = jnp.zeros(out_refs[k].shape, F32)
        for side in range(C):
            states = [states_refs[k][n % 2 * (Z // 2) + n // 2, at_ref[1] ^ side] for n in range(Z)]
            total = total + dot(jnp.concatenate(states, axis=0), piece_refs[side][...], ((0,), (0,)))
        out_refs[k][...] = total.astype(out_refs[k].dtype)


def add_kernel(at_ref, mine_ref, other_ref, out_ref):
    total = (mine_ref[...].astype(F32) + other_ref[...].astype(F32)).astype(BF)
    for n in range(out_ref.shape[0]):
        out_ref[n] = total


def local_call(kernel, shape, dtype, *operands):
    vmem = pl.BlockSpec(memory_space=pltpu.VMEM)
    return pl.pallas_call(
        kernel,
        out_shape=jax.ShapeDtypeStruct(shape, dtype),
        in_specs=[pl.BlockSpec(memory_space=pltpu.SMEM)] + [vmem] * (len(operands) - 1),
        out_specs=vmem,
        compiler_params=pltpu.CompilerParams(vmem_limit_bytes=40 * 1024 * 1024),
    )(*operands)


def weight_call(shape, *operands):
    vmem = pl.BlockSpec(memory_space=pltpu.VMEM)
    return pl.pallas_call(
        weight_kernel,
        out_shape=[jax.ShapeDtypeStruct(shape, BF)] * X,
        in_specs=[pl.BlockSpec(memory_space=pltpu.SMEM)] + [vmem] * (len(operands) - 1),
        out_specs=[vmem] * X,
        compiler_params=pltpu.CompilerParams(vmem_limit_bytes=40 * 1024 * 1024),
    )(*operands)


def gather(x, axis, size):
    copies = jnp.broadcast_to(x[None], (size,) + x.shape)
    return lax.all_to_all(copies, axis, 0, 0, tiled=True)


def swap(x, axis, size=2, bit=1):
    return lax.ppermute(x, axis, [(n, n ^ bit) for n in range(size)])


def body(states, qkv, grad_out, weight, offsets):
    rows, columns = qkv.shape
    half = rows // 2
    wide = GROUP * HEAD_DIM
    pair = 2 * HEAD_DIM
    core = lax.axis_index("c")
    mine = lax.axis_index("x")
    high = lax.axis_index("h")
    deep = high * (Z // 2) + lax.axis_index("l")
    where = jnp.stack([mine, core, high]).astype(jnp.int32)
    slab = jnp.arange(half, dtype=jnp.int32)
    starts = offsets.reshape(X, Z, C, 2)
    row_start = lax.dynamic_index_in_dim(lax.dynamic_index_in_dim(starts, deep, 1, False), core, 1, False)
    row_start = jnp.stack([lax.dynamic_index_in_dim(row_start, mine ^ k, 0, False) for k in range(X)])
    query_pos = (row_start[:, :, None] + slab).reshape(X, rows)
    query_pos = jnp.tile(query_pos, (1, GROUP))
    key_start = lax.dynamic_index_in_dim(starts, mine, 0, False)
    key_start = jnp.stack([lax.dynamic_index_in_dim(key_start, core ^ k, 1, False) for k in range(C)])
    key_start = jnp.moveaxis(key_start.reshape(C, 2, Z // 2, 2), 1, 2)
    key_pos = (key_start.reshape(-1)[:, None] + slab[None, :]).reshape(-1, 1)

    qg = jnp.concatenate([qkv[:, :wide], grad_out], axis=1)
    pairs = qkv[:, wide:]
    qg_x = [qg] + [swap(qg, "x", X, k) for k in range(1, X)]
    own = gather(pairs, ("l", "h"), Z).reshape(Z * rows, pair)
    own, key_pos, query_pos, *qg_x = lax.optimization_barrier((own, key_pos, query_pos, *qg_x))
    other = swap(own, "c")

    stats = attention_stats(own, other, key_pos, query_pos, qg_x)
    stats = lax.all_to_all(stats, "x", 0, 0, tiled=True)
    dq, dkv, dkv_give = attention_grads(where, stats, own, other, key_pos, query_pos, qg_x)

    dkv_in = swap(dkv_give, "c")
    dq = jnp.sum(lax.all_to_all(dq, "x", 0, 0, tiled=True).astype(F32), axis=0).astype(BF)
    dkv = (dkv.astype(F32) + dkv_in.astype(F32)).astype(BF)
    dkv, dq, weight, states = lax.optimization_barrier((dkv, dq, weight, states))
    depth = weight.shape[0]
    blocks = states.reshape(X, Z, C, rows, depth)
    blocks = [lax.dynamic_index_in_dim(blocks, mine ^ k, 0, keepdims=False) for k in range(X)]
    blocks = [blocks[0]] + [swap(blocks[k], "x", X, k) for k in range(1, X)]
    dkv = lax.all_to_all(dkv.reshape(Z // 2, 2, rows, pair), "l", 0, 0, tiled=True)
    dkv = jnp.sum(dkv.astype(F32), axis=0).astype(BF)
    joint = jnp.concatenate([dkv, dq[None, :, :pair], dq[None, :, pair:]], axis=0)
    grads = local_call(combine_kernel, (Z // 2, 2, rows, columns), BF, where, joint, swap(joint, "h"))
    grads, weight, *blocks = lax.optimization_barrier((grads, weight, *blocks))
    weights = [weight] + [swap(weight, "x", X, k) for k in range(1, X)]

    grads = lax.all_to_all(grads, "l", 0, 0, tiled=True).reshape(Z * rows, columns)
    grads, *weights = lax.optimization_barrier((grads, *weights))
    pieces = [grads, swap(grads, "c")]

    part = local_call(project_kernel, (X, Y, Z // Y, C, rows, depth), BF, where, *pieces, *weights)
    part = lax.all_to_all(part.reshape(X * Y, -1, depth), ("x", "y"), 0, 0, tiled=True)
    part = jnp.sum(part.reshape(X, Y, -1, depth).astype(F32), axis=1).astype(BF)
    part, *pieces = lax.optimization_barrier((part, *pieces))
    other = swap(part, "w")
    gw = weight_call((depth, columns), where, *pieces, *blocks)
    gw = [gw[0]] + [swap(gw[k], "x", X, k) for k in range(1, X)]
    part = local_call(add_kernel, (Y,) + part.shape, BF, where, part, other)
    part, *gw = lax.optimization_barrier((part, *gw))
    grad_states = lax.all_to_all(part, "y", 0, 0, tiled=True)
    grad_states, *gw = lax.optimization_barrier((grad_states, *gw))
    grad_weight = sum(piece.astype(F32) for piece in gw)
    return jnp.moveaxis(grad_states, 0, 1).reshape(-1, depth), grad_weight


def solution(mesh):
    fine = Mesh(mesh.devices.reshape(X, 2, Z // 2, C, W, Y), ("x", "h", "l", "c", "w", "y"))
    ctx, tp = ("x", "h", "l", "c"), ("w", "y")
    return jax.shard_map(
        body,
        mesh=fine,
        in_specs=(P(None, ctx), P(ctx, tp), P(ctx, tp), P(ctx, tp), P()),
        out_specs=(P(None, ctx), P(ctx, tp)),
        check_vma=False,
    )
```
